32 devices in a mesh: leaf: 8 (over z, x), win: 4 (over y, core).
Axes of the slice: x: 2, y: 2, z: 4, core: 2. Of those that a mesh axis runs over, the one named last changes fastest.
Arguments:
- blocks: float32 [8192, 256], P(('win', 'leaf')), parts along dimension 0, may hold values from 0 to 3, as said below
- factors: float32 [8192, 4, 256], P(('win', 'leaf')), parts along dimension 0, may hold values from -6 to 6
- targets: float32 [8192, 128], P(('win', 'leaf')), parts along dimension 0, may hold values from -6 to 6
Outputs:
- coarse: float32 [8192, 256], P(('win', 'leaf')), parts along dimension 0
- solution: float32 [8192, 128], P(('win', 'leaf')), parts along dimension 0
The draws below stay inside these ranges and needn't reach their ends.
There are 4 independent parts, one for each index of `win`. The reference program is written for one: setup_inputs(seed, part) draws one part's arguments, and reference() takes and returns one part's arrays. A program takes and returns all parts, laid end to end along the dimension named above; each array names one. Nothing has to cross between parts.
Inputs may be any that keep to these rules, and one draw needn't show every extreme that they name: `blocks`: every 256 x 256 block is symmetric positive definite.
All inputs are finite; a program needn't handle non-finite values.
Results may differ from the reference program's by a relative error of at most 0.0001.
Values sent between devices are 32-bit elements; how exact they have to be, the bound alone decides.
A program may use at most 64 MiB of HBM per device.

```python
import jax
import jax.numpy as jnp
from jax import lax

ROWS_DEV = 256
COUPLING = 256
NRHS = 128
LEVELS = 3
ROWS = 2048


def draw_blocks(key, part):
    count = ROWS // ROWS_DEV
    keys = jax.random.split(jax.random.fold_in(key, 11), 3)
    jitter = jax.random.uniform(keys[0], (count, ROWS_DEV, 2), jnp.float32, -1.0, 1.0)
    amp_raw = jax.random.uniform(keys[1], (count, ROWS_DEV), jnp.float32, -1.0, 1.0)
    nug_raw = jax.random.uniform(keys[2], (count, ROWS_DEV), jnp.float32, 0.0, 1.0)
    length = 2.5
    amplitude = jnp.exp(0.3 * amp_raw)
    nugget = 0.2 + 0.3 * nug_raw
    shake = 0.35
    position = jnp.arange(ROWS_DEV, dtype=jnp.int32)
    grid_row = (position // 16).astype(jnp.float32)
    grid_col = (position % 16).astype(jnp.float32)
    point_x = grid_row[None, :] + shake * jitter[:, :, 0]
    point_y = grid_col[None, :] + shake * jitter[:, :, 1]
    delta_x = point_x[:, :, None] - point_x[:, None, :]
    delta_y = point_y[:, :, None] - point_y[:, None, :]
    distance = jnp.sqrt(delta_x * delta_x + delta_y * delta_y)
    kernel = amplitude[:, :, None] * amplitude[:, None, :] * jnp.exp(-distance / length)
    on_diag = position[:, None] == position[None, :]
    block = kernel + jnp.where(on_diag[None], nugget[:, :, None], 0.0)
    return block.reshape(ROWS, ROWS_DEV).astype(jnp.float32)


def steps_of(own_key, shape, cuts, least, high):
    def one(axis_at, parts):
        steps = jax.random.uniform(jax.random.fold_in(jax.random.fold_in(own_key, 6), axis_at), (parts,), jnp.float32, least / len(cuts), high / len(cuts))
        return jnp.repeat(jnp.exp(steps), shape[axis_at] // parts).reshape((-1,) + (1,) * (len(shape) - axis_at - 1))

    loudness = one(*cuts[0])
    for cut in cuts[1:]:
        loudness = loudness * one(*cut)
    return loudness


def centred(stream_key, dims, scale, limit, cuts=(), kind=jnp.bfloat16):
    drawn = scale * jax.random.normal(stream_key, dims, jnp.float32)
    if cuts:
        drawn = drawn * steps_of(stream_key, dims, cuts, -0.22, 0.18)
    return jnp.clip(drawn, -limit, limit).astype(kind)


def setup_inputs(seed: int = 0, part: int = 0) -> dict:
    seeds = jax.random.split(jax.random.key(seed), 4)
    part_keys = jax.random.split(jax.random.fold_in(seeds[3], part), 4)
    blocks = draw_blocks(jax.random.fold_in(jax.random.fold_in(seeds[3], part), 71), part)
    factors = centred(part_keys[1], (ROWS, LEVELS + 1, COUPLING), 1.0, 6.0, ((0, 8),), jnp.float32)
    targets = centred(part_keys[2], (ROWS, NRHS), 1.0, 6.0, ((0, 8),), jnp.float32)
    return dict(blocks=blocks, factors=factors, targets=targets)


def leaf_solve(pair):
    block, columns = pair
    lower = jnp.linalg.cholesky(block)
    return jax.scipy.linalg.cho_solve((lower, True), columns)

def coupling_solve(pair):
    coupling, right = pair
    lower = jnp.linalg.cholesky(coupling)
    return jax.scipy.linalg.cho_solve((lower, True), right)

def reference(blocks, factors, targets):
    count = ROWS // ROWS_DEV
    width = COUPLING
    columns = jnp.concatenate([factors.reshape(ROWS, (LEVELS + 1) * width), targets], axis=1)
    solved = lax.map(leaf_solve, (blocks.reshape(count, ROWS_DEV, ROWS_DEV), columns.reshape(count, ROWS_DEV, -1)))
    basis_all = factors.reshape(count, ROWS_DEV, LEVELS + 1, width)
    identity = jnp.eye(width, dtype=jnp.float32)
    for height in range(LEVELS):
        group_size = 2 ** (height + 1)
        nodes = count // group_size
        weight = 1.0 / (group_size * ROWS_DEV)
        node_rows = solved.reshape(nodes, group_size * ROWS_DEV, -1)
        basis_rows = basis_all[:, :, height, :].reshape(nodes, group_size * ROWS_DEV, width)
        panels = jnp.einsum('nrk,nrc->nkc', basis_rows, node_rows, precision=lax.Precision.HIGHEST)
        couplings = identity[None] + weight * panels[:, :, :width]
        update = lax.map(coupling_solve, (couplings, weight * panels[:, :, width:]))
        remaining = node_rows[:, :, width:] - jnp.einsum('nrk,nkc->nrc', node_rows[:, :, :width], update, precision=lax.Precision.HIGHEST)
        solved = remaining.reshape(count, ROWS_DEV, -1)
    final = solved.reshape(ROWS, -1)
    return (final[:, :width], final[:, width:])
```

```python
import functools

import jax
import jax.numpy as jnp
from jax import lax
from jax.experimental import pallas as pl
from jax.experimental.pallas import tpu as pltpu
from jax.sharding import PartitionSpec as P

LEVELS = 3
PIVOTS = 16
LANES = 128
VMEM_LIMIT = 48 * 2**20


def dot(left, right, dims=((1,), (0,))):
    return lax.dot_general(
        left,
        right,
        (dims, ((), ())),
        precision=lax.Precision.HIGHEST,
        preferred_element_type=jnp.float32,
    )


def eliminate(rows, first):
    count, width = rows.shape
    sub = lax.broadcasted_iota(jnp.int32, (count, LANES), 0)
    lane = lax.broadcasted_iota(jnp.int32, (count, LANES), 1)
    pivot_cols = [
        jnp.broadcast_to(rows[:, first + k : first + k + 1], (count, LANES)) for k in range(count)
    ]
    tiles = []
    for start in range(0, width, LANES):
        tile = rows[:, start : start + LANES]
        if start <= first < start + LANES:
            offset = lane - (first - start)
            inside = (offset >= 0) & (offset < count)
            tile = jnp.where(inside, jnp.where(offset == sub, 1.0, 0.0), tile)
        tiles.append(tile)
    for k in range(count):
        column = pivot_cols[k]
        scale = 1.0 / column[k : k + 1, :]
        is_pivot = sub == k

        def step(tile):
            top = tile[k : k + 1, :] * scale
            return jnp.where(is_pivot, top, tile - column * top)

        for j in range(k + 1, count):
            pivot_cols[j] = step(pivot_cols[j])
        tiles = [step(tile) for tile in tiles]
    return jnp.concatenate(tiles, axis=1)


def invert(a_ref):
    order = a_ref.shape[0]
    lane = lax.broadcasted_iota(jnp.int32, (PIVOTS, order), 1)
    lane_all = lax.broadcasted_iota(jnp.int32, (order, order), 1)
    for first in range(0, order, PIVOTS):
        rows = a_ref[first : first + PIVOTS, :]
        swept = eliminate(rows, first)
        inside = (lane >= first) & (lane < first + PIVOTS)
        outer = jnp.where(inside, 0.0, rows)
        swept = jnp.where(inside, -swept, swept)
        inside_all = (lane_all >= first) & (lane_all < first + PIVOTS)
        a_ref[...] = jnp.where(inside_all, 0.0, a_ref[...]) - dot(outer, swept, ((0,), (0,)))
        a_ref[first : first + PIVOTS, :] = swept


def leaf_kernel(block_ref, factors_hbm, targets_ref, y_ref, gram_ref, pieces_ref, basis_ref, work, cols, sems):
    coupling = factors_hbm.shape[2]
    count = factors_hbm.shape[1]
    copies = []
    for h in range(count):
        copy = pltpu.make_async_copy(
            factors_hbm.at[:, h, :], cols.at[:, h * coupling : (h + 1) * coupling], sems.at[h]
        )
        copy.start()
        copies.append(copy)
    work[...] = block_ref[...]
    invert(work)
    for copy in copies:
        copy.wait()
    cols[:, count * coupling :] = targets_ref[...]
    y_ref[...] = -dot(work[...], cols[...])
    basis = cols[:, :coupling]
    gram_ref[...] = dot(basis, y_ref[:, :coupling], ((0,), (0,)))
    pieces_ref[...] = dot(basis, y_ref[:, coupling:], ((0,), (0,)))
    basis_ref[...] = cols[:, coupling : LEVELS * coupling]


def inverse_kernel(weight, gram_ref, out_ref):
    order = gram_ref.shape[0]
    row = lax.broadcasted_iota(jnp.int32, (order, order), 0)
    col = lax.broadcasted_iota(jnp.int32, (order, order), 1)
    out_ref[...] = jnp.where(row == col, 1.0, 0.0) + weight * gram_ref[...]
    invert(out_ref)


def update_kernel(weight, y_ref, inverse_ref, pieces_ref, basis_ref, out_ref, gram_ref, next_ref):
    coupling = inverse_ref.shape[0]
    solved = dot(inverse_ref[...], weight * pieces_ref[...])
    out_ref[...] = y_ref[:, coupling:] + dot(y_ref[:, :coupling], solved)
    basis = basis_ref[...]
    gram_ref[...] = dot(basis, out_ref[:, :coupling], ((0,), (0,)))
    next_ref[...] = dot(basis, out_ref[:, coupling:], ((0,), (0,)))


def last_kernel(weight, y_ref, inverse_ref, pieces_ref, coarse_ref, solution_ref):
    coupling = inverse_ref.shape[0]
    solved = dot(inverse_ref[...], weight * pieces_ref[...])
    final = y_ref[:, coupling:] + dot(y_ref[:, :coupling], solved)
    coarse_ref[...] = final[:, :coupling]
    solution_ref[...] = final[:, coupling:]


def call(kernel, shapes, args, in_specs=None, scratch=()):
    vmem = pl.BlockSpec(memory_space=pltpu.VMEM)
    flops = sum(2 * 6 * 256 * s[0] * s[1] for s in shapes)
    return pl.pallas_call(
        kernel,
        out_shape=[jax.ShapeDtypeStruct(s, jnp.float32) for s in shapes],
        in_specs=in_specs or [vmem] * len(args),
        out_specs=[vmem] * len(shapes),
        scratch_shapes=list(scratch),
        cost_estimate=pl.CostEstimate(flops=max(flops, 10**10), bytes_accessed=4 * 10**6, transcendentals=0),
        compiler_params=pltpu.CompilerParams(vmem_limit_bytes=VMEM_LIMIT),
    )(*args)


def from_partner(array, axis, apart):
    return lax.ppermute(array, axis, [(i, i ^ 1 << apart) for i in range(lax.axis_size(axis))])


def summed(pieces, height, leaf_index):
    for which_bit in range(height + 1):
        half_cols = pieces.shape[1] // 2
        lower_half = pieces[:, :half_cols]
        upper_half = pieces[:, half_cols:]
        is_upper = leaf_index >> which_bit & 1 == 1
        outgoing = jnp.where(is_upper, lower_half, upper_half)
        kept = jnp.where(is_upper, upper_half, lower_half)
        pieces = kept + from_partner(outgoing, "leaf", which_bit)
    for which_bit in reversed(range(height + 1)):
        partner = from_partner(pieces, "leaf", which_bit)
        is_upper = leaf_index >> which_bit & 1 == 1
        pieces = jnp.where(
            is_upper,
            jnp.concatenate([partner, pieces], axis=1),
            jnp.concatenate([pieces, partner], axis=1),
        )
    return pieces


def shards(blocks, factors, targets):
    rows = blocks.shape[0]
    coupling = factors.shape[2]
    count = factors.shape[1]
    rhs = targets.shape[1]
    width = count * coupling + rhs
    leaf_index = lax.axis_index("leaf")
    vmem = pl.BlockSpec(memory_space=pltpu.VMEM)
    y, gram, pieces, basis = call(
        leaf_kernel,
        [(rows, width), (coupling, coupling), (coupling, width - coupling), (rows, (LEVELS - 1) * coupling)],
        (blocks, factors, targets),
        [vmem, pl.BlockSpec(memory_space=pl.ANY), vmem],
        [
            pltpu.VMEM((rows, rows), jnp.float32),
            pltpu.VMEM((rows, width), jnp.float32),
            pltpu.SemaphoreType.DMA((count,)),
        ],
    )
    for height in range(LEVELS):
        weight = 1.0 / (2 ** (height + 1) * rows)
        for which_bit in range(height + 1):
            gram = gram + from_partner(gram, "leaf", which_bit)
        if height == 0:
            pieces = pieces + from_partner(pieces, "leaf", 0)
        else:
            pieces = summed(pieces, height, leaf_index)
        (inverse,) = call(functools.partial(inverse_kernel, weight), [(coupling, coupling)], (gram,))
        width -= coupling
        if height < LEVELS - 1:
            y, gram, pieces = call(
                functools.partial(update_kernel, weight),
                [(rows, width), (coupling, coupling), (coupling, width - coupling)],
                (y, inverse, pieces, basis[:, height * coupling : (height + 1) * coupling]),
            )
        else:
            coarse, answer = call(
                functools.partial(last_kernel, weight),
                [(rows, coupling), (rows, rhs)],
                (y, inverse, pieces),
            )
    return coarse, answer


def solution(mesh):
    placed = (P(("win", "leaf"), None), P(("win", "leaf"), None, None), P(("win", "leaf"), None))
    return jax.shard_map(
        shards,
        mesh=mesh,
        in_specs=placed,
        out_specs=(P(("win", "leaf"), None), P(("win", "leaf"), None)),
        check_vma=False,
    )
```

```python
import functools

import jax
import jax.numpy as jnp
from jax import lax
from jax.experimental import pallas as pl
from jax.experimental.pallas import tpu as pltpu
from jax.sharding import PartitionSpec as P

LEVELS = 3
PIVOTS = 16
LANES = 128
VMEM_LIMIT = 48 * 2**20


def dot(left, right, dims=((1,), (0,))):
    return lax.dot_general(
        left,
        right,
        (dims, ((), ())),
        precision=lax.Precision.HIGHEST,
        preferred_element_type=jnp.float32,
    )


def eliminate(rows, first):
    count, width = rows.shape
    sub = lax.broadcasted_iota(jnp.int32, (count, LANES), 0)
    lane = lax.broadcasted_iota(jnp.int32, (count, LANES), 1)
    pivot_cols = [
        jnp.broadcast_to(rows[:, first + k : first + k + 1], (count, LANES)) for k in range(count)
    ]
    tiles = []
    for start in range(0, width, LANES):
        tile = rows[:, start : start + LANES]
        if start <= first < start + LANES:
            offset = lane - (first - start)
            inside = (offset >= 0) & (offset < count)
            tile = jnp.where(inside, jnp.where(offset == sub, 1.0, 0.0), tile)
        tiles.append(tile)
    for k in range(count):
        column = pivot_cols[k]
        scale = 1.0 / column[k : k + 1, :]
        is_pivot = sub == k

        def step(tile):
            top = tile[k : k + 1, :] * scale
            return jnp.where(is_pivot, top, tile - column * top)

        for j in range(k + 1, count):
            pivot_cols[j] = step(pivot_cols[j])
        tiles = [step(tile) for tile in tiles]
    return jnp.concatenate(tiles, axis=1)


def invert(a_ref, between=lambda block: None):
    order = a_ref.shape[0]
    lane = lax.broadcasted_iota(jnp.int32, (PIVOTS, order), 1)
    lane_all = lax.broadcasted_iota(jnp.int32, (order, order), 1)
    for first in range(0, order, PIVOTS):
        rows = a_ref[first : first + PIVOTS, :]
        swept = eliminate(rows, first)
        inside = (lane >= first) & (lane < first + PIVOTS)
        outer = jnp.where(inside, 0.0, rows)
        swept = jnp.where(inside, -swept, swept)
        inside_all = (lane_all >= first) & (lane_all < first + PIVOTS)
        a_ref[...] = jnp.where(inside_all, 0.0, a_ref[...]) - dot(outer, swept, ((0,), (0,)))
        a_ref[first : first + PIVOTS, :] = swept
        between(first // PIVOTS)


def leaf_kernel(block_ref, factors_hbm, targets_ref, y_ref, gram_ref, pieces_ref, basis_ref, work, cols, sems):
    coupling = factors_hbm.shape[2]
    count = factors_hbm.shape[1]
    copies = []
    for h in range(count):
        copy = pltpu.make_async_copy(
            factors_hbm.at[:, h, :], cols.at[:, h * coupling : (h + 1) * coupling], sems.at[h]
        )
        copy.start()
        copies.append(copy)
    work[...] = block_ref[...]
    invert(work)
    for copy in copies:
        copy.wait()
    cols[:, count * coupling :] = targets_ref[...]
    y_ref[...] = -dot(work[...], cols[...])
    basis = cols[:, :coupling]
    gram_ref[...] = dot(basis, y_ref[:, :coupling], ((0,), (0,)))
    pieces_ref[...] = dot(basis, y_ref[:, coupling:], ((0,), (0,)))
    basis_ref[...] = cols[:, coupling : LEVELS * coupling]


class Exchange:
    def __init__(self, src, total, acc, inbox, send_sems, recv_sems, span, order):
        self.src, self.total, self.acc, self.inbox = src, total, acc, inbox
        self.send_sems, self.recv_sems, self.order = send_sems, recv_sems, order
        self.span = span
        self.me = lax.axis_index("leaf")
        self.rows = src.shape[0]
        self.begins = [0]
        for s, bit in enumerate(order):
            self.begins.append(self.begins[-1] + (self.me // 2**bit % 2) * (self.rows >> s + 1))
        self.steps = 2 * len(order)
        self.copy = None
        self.done = 0

    def at(self, ref, begin, size, local=True):
        columns = self.span if local else slice(None)
        return ref.at[pl.ds(pl.multiple_of(begin, size), size), columns]

    def partner(self, bit):
        low = self.me // 2**bit % 2
        return self.me + (1 - 2 * low) * 2**bit

    def start(self):
        s, n = self.done, len(self.order)
        if s < n:
            size = self.rows >> s + 1
            kept = self.begins[s + 1]
            sent = 2 * self.begins[s] + size - kept
            source = self.at(self.src if s == 0 else self.acc, sent, size)
            target = self.inbox.at[pl.ds(self.rows - 2 * size, size), self.span]
            bit = self.order[s]
        else:
            level = 2 * n - s
            size = self.rows >> level
            source = self.at(self.total, self.begins[level], size)
            target = source
            bit = self.order[level - 1]
        self.copy = pltpu.make_async_remote_copy(
            src_ref=source,
            dst_ref=target,
            send_sem=self.send_sems.at[s],
            recv_sem=self.recv_sems.at[s],
            device_id={"leaf": self.partner(bit)},
            device_id_type=pl.DeviceIdType.MESH,
        )
        self.copy.start()

    def finish(self):
        s, n = self.done, len(self.order)
        self.copy.wait()
        if s < n:
            size = self.rows >> s + 1
            kept = self.begins[s + 1]
            own = self.at(self.src if s == 0 else self.acc, kept, size)[...]
            other = self.inbox[pl.ds(self.rows - 2 * size, size), self.span]
            self.at(self.acc if s < n - 1 else self.total, kept, size)[...] = own + other
        self.done += 1


class Swap:
    def __init__(self, src, total, inbox, send_sem, recv_sem):
        self.src, self.total, self.inbox = src, total, inbox
        self.steps = 1
        me = lax.axis_index("leaf")
        self.copy = pltpu.make_async_remote_copy(
            src_ref=src,
            dst_ref=inbox,
            send_sem=send_sem,
            recv_sem=recv_sem,
            device_id={"leaf": me + 1 - 2 * (me % 2)},
            device_id_type=pl.DeviceIdType.MESH,
        )

    def start(self):
        self.copy.start()

    def finish(self):
        self.copy.wait()
        self.total[...] = self.src[...] + self.inbox[...]


def couple_kernel(
    weight, height, gram_ref, pieces_ref, inverse_ref, sum_ref,
    gram_total, gram_acc, gram_inbox, total, acc, inbox, send_sems, recv_sems,
):
    me = lax.axis_index("leaf")
    barrier = pltpu.get_barrier_semaphore()
    for bit in range(height + 1):
        low = me // 2**bit % 2
        pl.semaphore_signal(
            barrier, inc=1, device_id={"leaf": me + (1 - 2 * low) * 2**bit}, device_id_type=pl.DeviceIdType.MESH
        )
    pl.semaphore_wait(barrier, height + 1)
    order = gram_ref.shape[0]
    if height == 0:
        grams = [Swap(gram_ref, gram_total, gram_inbox, send_sems.at[0, 0], recv_sems.at[0, 0])]
        panels = [Swap(pieces_ref, total, inbox, send_sems.at[1, 0], recv_sems.at[1, 0])]
    else:
        orders = [list(range(height + 1)), [1, 0] + list(range(2, height + 1))]
        cut = order // 2
        grams = [
            Exchange(gram_ref, gram_total, gram_acc, gram_inbox, send_sems.at[i], recv_sems.at[i], span, orders[i])
            for i, span in enumerate([slice(0, cut), slice(cut, order)])
        ]
        width = pieces_ref.shape[1]
        cut = width // 2 // LANES * LANES
        panels = [
            Exchange(pieces_ref, total, acc, inbox, send_sems.at[2 + i], recv_sems.at[2 + i], span, orders[i])
            for i, span in enumerate([slice(0, cut), slice(cut, width)])
        ]
    for step in range(grams[0].steps):
        for each in grams:
            each.start()
        if step == grams[0].steps - 1:
            for each in panels:
                each.start()
        for each in grams:
            each.finish()
    row = lax.broadcasted_iota(jnp.int32, (order, order), 0)
    col = lax.broadcasted_iota(jnp.int32, (order, order), 1)
    inverse_ref[...] = jnp.where(row == col, 1.0, 0.0) + weight * gram_total[...]
    steps = panels[0].steps
    blocks = order // PIVOTS

    def between(block):
        for step in range(steps):
            if block == min((step + 1) * blocks // steps, blocks) - 1:
                for each in panels:
                    each.finish()
                if step < steps - 1:
                    for each in panels:
                        each.start()

    invert(inverse_ref, between)
    sum_ref[...] = total[...]


def update_kernel(weight, y_ref, inverse_ref, pieces_ref, basis_ref, out_ref, gram_ref, next_ref):
    coupling = inverse_ref.shape[0]
    solved = dot(inverse_ref[...], weight * pieces_ref[...])
    out_ref[...] = y_ref[:, coupling:] + dot(y_ref[:, :coupling], solved)
    basis = basis_ref[...]
    gram_ref[...] = dot(basis, out_ref[:, :coupling], ((0,), (0,)))
    next_ref[...] = dot(basis, out_ref[:, coupling:], ((0,), (0,)))


def last_kernel(weight, y_ref, inverse_ref, pieces_ref, coarse_ref, solution_ref):
    coupling = inverse_ref.shape[0]
    solved = dot(inverse_ref[...], weight * pieces_ref[...])
    final = y_ref[:, coupling:] + dot(y_ref[:, :coupling], solved)
    coarse_ref[...] = final[:, :coupling]
    solution_ref[...] = final[:, coupling:]


def call(kernel, shapes, args, in_specs=None, scratch=(), **params):
    vmem = pl.BlockSpec(memory_space=pltpu.VMEM)
    flops = sum(2 * 6 * 256 * s[0] * s[1] for s in shapes)
    return pl.pallas_call(
        kernel,
        out_shape=[jax.ShapeDtypeStruct(s, jnp.float32) for s in shapes],
        in_specs=in_specs or [vmem] * len(args),
        out_specs=[vmem] * len(shapes),
        scratch_shapes=list(scratch),
        cost_estimate=pl.CostEstimate(flops=max(flops, 10**10), bytes_accessed=4 * 10**6, transcendentals=0),
        compiler_params=pltpu.CompilerParams(vmem_limit_bytes=VMEM_LIMIT, **params),
    )(*args)


def shards(blocks, factors, targets):
    rows = blocks.shape[0]
    coupling = factors.shape[2]
    count = factors.shape[1]
    rhs = targets.shape[1]
    width = count * coupling + rhs
    vmem = pl.BlockSpec(memory_space=pltpu.VMEM)
    y, gram, pieces, basis = call(
        leaf_kernel,
        [(rows, width), (coupling, coupling), (coupling, width - coupling), (rows, (LEVELS - 1) * coupling)],
        (blocks, factors, targets),
        [vmem, pl.BlockSpec(memory_space=pl.ANY), vmem],
        [
            pltpu.VMEM((rows, rows), jnp.float32),
            pltpu.VMEM((rows, width), jnp.float32),
            pltpu.SemaphoreType.DMA((count,)),
        ],
    )
    for height in range(LEVELS):
        weight = 1.0 / (2 ** (height + 1) * rows)
        panel = pieces.shape
        square = (coupling, coupling)
        inverse, pieces = call(
            functools.partial(couple_kernel, weight, height),
            [square, panel],
            (gram, pieces),
            None,
            [pltpu.VMEM(square, jnp.float32)] * 3
            + [pltpu.VMEM(panel, jnp.float32)] * 3
            + [pltpu.SemaphoreType.DMA((4, 2 * (height + 1)))] * 2,
            collective_id=height,
            has_side_effects=True,
        )
        width -= coupling
        if height < LEVELS - 1:
            y, gram, pieces = call(
                functools.partial(update_kernel, weight),
                [(rows, width), (coupling, coupling), (coupling, width - coupling)],
                (y, inverse, pieces, basis[:, height * coupling : (height + 1) * coupling]),
            )
        else:
            coarse, answer = call(
                functools.partial(last_kernel, weight),
                [(rows, coupling), (rows, rhs)],
                (y, inverse, pieces),
            )
    return coarse, answer


def solution(mesh):
    placed = (P(("win", "leaf"), None), P(("win", "leaf"), None, None), P(("win", "leaf"), None))
    return jax.shard_map(
        shards,
        mesh=mesh,
        in_specs=placed,
        out_specs=(P(("win", "leaf"), None), P(("win", "leaf"), None)),
        check_vma=False,
    )
```
